256 devices in a mesh: row: 32 (over z, x_lo, core), col: 8 (over y, x_hi).
Axes of the slice: x: 4 (x_hi: 2, x_lo: 2; x = x_hi * 2 + x_lo), y: 4, z: 8, core: 2. Of those that a mesh axis runs over, the one named last changes fastest.
Arguments:
- activations: bfloat16 [768, 28672], P('row', 'col'), may hold values from -6 to 6
- out_grads: bfloat16 [768, 8192], P('col', 'row'), may hold values from -0.3046875 to 0.3046875
- in_basis: bfloat16 [28672, 28672], P('col', 'row'), may hold values from -0.03125 to 0.03125
- out_basis: bfloat16 [8192, 8192], P('row', 'col'), may hold values from -0.0625 to 0.0625
Outputs:
- correction: float32 [28672, 8192], P('row', 'col')
The draws below stay inside these ranges and needn't reach their ends.
All inputs are finite; a program needn't handle non-finite values.
Results may differ from the reference program's by a relative error of at most 0.0042.
Values may be sent and summed in bfloat16 or wider, within the bound.
A program may use at most 64 MiB of HBM per device.

```python
import jax
import jax.numpy as jnp
from jax import lax

IN = 28672
OUT = 8192
SEQ_LEN = 384
SEQS = 2
TOKENS = 768


def level_of(key, dims, cuts, low, top_value):
    gain = 1.0
    for dim, shards_of in cuts:
        steps = jax.random.uniform(jax.random.fold_in(jax.random.fold_in(key, 6), dim), (shards_of,), jnp.float32, low / len(cuts), top_value / len(cuts))
        gain = gain * jnp.repeat(jnp.exp(steps), dims[dim] // shards_of).reshape((-1,) + (1,) * (len(dims) - 1 - dim))
    return gain


def normal_values(stream_key, dims, width, reach, pieces=(), kind=jnp.bfloat16):
    drawn = jax.random.normal(stream_key, dims, jnp.float32) * width
    if len(pieces) > 0:
        drawn = level_of(stream_key, dims, pieces, -0.22, 0.18) * drawn
    return jnp.clip(drawn, min=-reach, max=reach).astype(kind)


def setup_inputs(seed: int = 0) -> dict:
    splits = jax.random.split(jax.random.key(seed), 5)
    return {
        "activations": normal_values(splits[0], (TOKENS, IN), 1.0, 6.0, ((0, 32), (1, 8))),
        "out_grads": normal_values(splits[1], (TOKENS, OUT), (SEQ_LEN ** -0.5), 0.3046875, ((0, 8), (1, 32))),
        "in_basis": normal_values(splits[2], (IN, IN), IN ** -0.5, 0.03125, ((0, 8), (1, 32))),
        "out_basis": normal_values(splits[3], (OUT, OUT), OUT ** -0.5, 0.0625, ((0, 32), (1, 8))),
    }


def reference(activations, out_grads, in_basis, out_basis):
    act_rotated = jnp.dot(activations, in_basis, preferred_element_type=jnp.float32).astype(jnp.bfloat16)
    grad_rotated = jnp.dot(out_grads, out_basis, preferred_element_type=jnp.float32).astype(jnp.bfloat16)
    accumulated = jnp.zeros((act_rotated.shape[1], grad_rotated.shape[1]), jnp.float32)
    for number in range(SEQS):
        act_seq = act_rotated[number * SEQ_LEN:(number + 1) * SEQ_LEN]
        grad_seq = grad_rotated[number * SEQ_LEN:(number + 1) * SEQ_LEN]
        seq_tile = lax.dot_general(act_seq, grad_seq, (((0,), (0,)), ((), ())), preferred_element_type=jnp.float32)
        accumulated = accumulated + seq_tile * seq_tile
    return accumulated / jnp.float32(SEQS)
```

```python
import functools

import jax
import jax.numpy as jnp
from jax import lax
from jax.experimental import pallas as pl
from jax.experimental.pallas import tpu as pltpu
from jax.sharding import PartitionSpec as P

MESH = pl.DeviceIdType.MESH
F32 = jnp.float32
BF16 = jnp.bfloat16
NZ, NY = 8, 4
COPIES = 180
VMEM_LIMIT = 58 * 2**20


def ring(value, size):
    return lax.rem(value + size, size)


def exchange(
    act_ref, grad_ref, in_basis, out_basis, act_out, grad_out,
    basis, obasis, pair, acts, part, send_y, recv_y, own_y, half_x, recv_x, done_x, rot_raw, rot,
    grads, gsend, grecv, gown, gx_send, gx_recv, gsum, ring_send, ring_recv, grot,
    send_sem, recv_sem, local_sem,
):
    row, col = lax.axis_index("row"), lax.axis_index("col")
    z, xl, core = row // 4, lax.rem(row // 2, 2), lax.rem(row, 2)
    y, xh = col // 2, lax.rem(col, 2)

    def at(z=z, xl=xl, core=core, y=y, xh=xh):
        return (z * 4 + xl * 2 + core, y * 2 + xh)

    sibling, beside, across = at(core=1 - core), at(xl=1 - xl), at(xh=1 - xh)
    up = (at(z=ring(z + 1, NZ)), at(z=ring(z - 1, NZ)))
    around = [at(y=ring(y + rel, NY)) for rel in (1, 2, 3)]
    ids, sent = {}, []

    def copy(key, src, dst, device):
        number = ids.setdefault(key, len(ids))
        return pltpu.make_async_remote_copy(
            src_ref=src, dst_ref=dst, send_sem=send_sem.at[number], recv_sem=recv_sem.at[number],
            device_id=device, device_id_type=MESH,
        )

    def send(key, src, dst, device):
        one = copy(key, src, dst, device)
        one.start()
        sent.append(one)

    def arrive(key, dst):
        copy(key, dst, dst, sibling).wait_recv()

    load_basis = pltpu.make_async_copy(in_basis, basis, local_sem.at[0])
    load_obasis = pltpu.make_async_copy(out_basis, obasis, local_sem.at[1])
    load_obasis.start()
    load_basis.start()

    barrier = pltpu.get_barrier_semaphore()
    near = [sibling, beside, across, *up, *around]
    for device in near:
        pl.semaphore_signal(barrier, inc=1, device_id=device, device_id_type=MESH)
    half = act_ref.shape[1] // 2
    quarter = half // 2
    mine = act_ref[...].astype(F32)
    for number in range(2):
        pair[2 + number] = mine[:, number * half : (number + 1) * half]
    pair[core] = pair[2 + core]
    grads[col] = grad_ref[...]
    pl.semaphore_wait(barrier, len(near))

    send("pair", pair.at[3 - core], pair.at[core], sibling)

    send(("g1", 0), grads.at[col], grads.at[col], across)
    for rel in (1, 2, 3):
        send(("g1", rel, 0), grads.at[col], grads.at[col], around[rel - 1])

    arrive("pair", pair.at[1 - core])

    def act_slot(zz, q, part_no, side=0):
        kk = core if side == 0 else 1 - core
        return acts.at[kk, part_no, zz, xl if q == 0 else 1 - xl]

    def grad_slot(zz, q, part_no, side=0):
        kk = core if side == 0 else 1 - core
        return grot.at[2 * kk + (xl if q == 0 else 1 - xl), zz, pl.ds(96 * part_no, 96)]

    def place(zoff):
        return ring(z + zoff, NZ)

    def gather_put(name, slot, q, part_no):
        ref = slot(z, q, part_no)
        for way in (0, 1):
            send((name, way, 1, q, part_no), ref, ref, up[way])
        if q == 0:
            send((name, "x", part_no), ref, ref, beside)
        send((name, "sib", 0, q, part_no), ref, ref, sibling)

    def gather_beside(name, slot, part_no):
        arrive((name, "x", part_no), slot(z, 1, part_no))
        gather_put(name, slot, 1, part_no)

    def gather_step(name, slot, step, way, q, part_no):
        if step == 4 and part_no != way:
            return
        zoff = -step if way == 0 else step
        ref = slot(place(zoff), q, part_no)
        arrive((name, way, step, q, part_no), ref)
        if step < 3 or (step == 3 and part_no == way):
            send((name, way, step + 1, q, part_no), ref, ref, up[way])
        send((name, "sib", 4 if step == 4 else zoff, q, part_no), ref, ref, sibling)

    def gather_steps(name, slot, step):
        for q in (0, 1):
            for part_no in (0, 1):
                for way in (0, 1):
                    gather_step(name, slot, step, way, q, part_no)

    def gather_sibling(name, slot, zoff):
        for q in (0, 1):
            for part_no in (0, 1):
                arrive((name, "sib", zoff, q, part_no), slot(place(zoff), q, part_no, 1))

    block = pair[0:2].reshape(48, half).astype(BF16)
    for part_no in (0, 1):
        acts[core, part_no, z, xl] = block[:, part_no * quarter : (part_no + 1) * quarter]
    for part_no in (0, 1):
        gather_put("a", act_slot, 0, part_no)

    other = y * 2 + 1 - xh
    arrive(("g1", 0), grads.at[other])
    for rel in (1, 2, 3):
        send(("g1", rel, 1), grads.at[other], grads.at[other], around[rel - 1])
    for part_no in (0, 1):
        gather_beside("a", act_slot, part_no)

    for rel in (1, 2, 3):
        came = ring(y - rel, NY) * 2
        arrive(("g1", rel, 0), grads.at[came + xh])
        arrive(("g1", rel, 1), grads.at[came + 1 - xh])

    load_obasis.wait()

    def partial(seq, ref):
        got = jnp.dot(grads[pl.ds(4 * seq, 4)].reshape(384, 256), obasis[...], preferred_element_type=F32)
        for side in range(2):
            for zc in range(NZ):
                ref[side, zc] = got[192 * side : 192 * side + 192, 128 * zc : 128 * zc + 128]

    partial(1 - core, gsend)
    send("g2core", gsend, grecv, sibling)
    partial(core, gown)
    load_basis.wait()

    def chunk(j):
        za, zb = place(-j), place(j + 1)
        if j == 0:
            gather_sibling("a", act_slot, 0)
        else:
            gather_sibling("a", act_slot, -j)
        gather_sibling("a", act_slot, j + 1)
        left = jnp.concatenate(
            [
                jnp.concatenate([acts[kk, pp, za].reshape(96, quarter), acts[kk, pp, zb].reshape(96, quarter)], axis=0)
                for kk in (0, 1)
                for pp in (0, 1)
            ],
            axis=1,
        )
        part[...] = jnp.dot(left, basis[...], preferred_element_type=F32).reshape(part.shape)
        for rel in (1, 2, 3):
            send_y[j, rel - 1] = part[ring(y + rel, NY)].astype(BF16)
            send(("s2", j, rel), send_y.at[j, rel - 1], recv_y.at[j, rel - 1], around[rel - 1])
        own_y[j] = part[y]

    def sum_y(j):
        total = own_y[j]
        for rel in (1, 2, 3):
            arrive(("s2", j, rel), recv_y.at[j, rel - 1])
            total = total + recv_y[j, rel - 1].astype(F32)
        half_x[j] = total.reshape(2, 24, -1)
        send(("s2x", j), half_x.at[j, 1 - xh], recv_x.at[j], across)

    def sum_x(j):
        arrive(("s2x", j), recv_x.at[j])
        done_x[j // 2, pl.ds(24 * (j % 2), 24)] = half_x[j, xh] + recv_x[j]

    def spread(p):
        rot_raw[p, y, xh] = done_x[p].astype(BF16)
        ref = rot_raw.at[p, y, xh]
        for rel in (1, 2, 3):
            send(("s3", p, rel, 0), ref, ref, around[rel - 1])
        send(("s3", p), ref, ref, across)

    def spread_on(p):
        ref = rot_raw.at[p, y, 1 - xh]
        arrive(("s3", p), ref)
        for rel in (1, 2, 3):
            send(("s3", p, rel, 1), ref, ref, around[rel - 1])

    def collect(p):
        for rel in (1, 2, 3):
            came = ring(y - rel, NY)
            arrive(("s3", p, rel, 0), rot_raw.at[p, came, xh])
            arrive(("s3", p, rel, 1), rot_raw.at[p, came, 1 - xh])
        whole = rot_raw[p].astype(F32)
        for odd in (0, 1):
            j = 2 * p + odd
            piece = whole[:, :, 24 * odd : 24 * odd + 24, :]
            rot[place(-j)] = piece[0:2].reshape(96, -1).astype(BF16)
            rot[place(j + 1)] = piece[2:4].reshape(96, -1).astype(BF16)

    def grad_beside():
        arrive("g2core", grecv)
        gx_send[...] = (gown[1 - xl] + grecv[1 - xl]).astype(BF16)
        send("g2x", gx_send, gx_recv, beside)

    def grad_sum():
        arrive("g2x", gx_recv)
        gsum[...] = gown[xl] + grecv[xl] + gx_recv[...].astype(F32)

    def length(way, part_no):
        return 4 if way == part_no else 3

    def grad_ring(step):
        for way in (0, 1):
            sign = 1 if way == 0 else -1
            for part_no in (0, 1):
                hops = length(way, part_no)
                if step > hops:
                    continue
                dest = place(sign * (hops - step + 1))
                value = gsum[dest, pl.ds(96 * part_no, 96)]
                if step > 1:
                    arrive(("g2", way, part_no, step - 1), ring_recv.at[way, part_no, step - 2])
                    value = value + ring_recv[way, part_no, step - 2]
                ring_send[way, part_no, step - 1] = value
                send(
                    ("g2", way, part_no, step),
                    ring_send.at[way, part_no, step - 1],
                    ring_recv.at[way, part_no, step - 1],
                    up[way],
                )

    def grad_end():
        for part_no in (0, 1):
            value = gsum[z, pl.ds(96 * part_no, 96)]
            for way in (0, 1):
                hops = length(way, part_no)
                arrive(("g2", way, part_no, hops), ring_recv.at[way, part_no, hops - 1])
                value = value + ring_recv[way, part_no, hops - 1]
            grot[2 * core + xl, z, pl.ds(96 * part_no, 96)] = value.astype(BF16)
        for part_no in (0, 1):
            gather_put("g", grad_slot, 0, part_no)

    gather_steps("a", act_slot, 1)
    grad_beside()
    chunk(0)
    gather_steps("a", act_slot, 2)
    sum_y(0)
    chunk(1)
    grad_sum()
    grad_ring(1)
    sum_x(0)
    gather_steps("a", act_slot, 3)
    sum_y(1)
    grad_ring(2)
    chunk(2)
    sum_x(1)
    spread(0)
    gather_steps("a", act_slot, 4)
    spread_on(0)
    sum_y(2)
    grad_ring(3)
    chunk(3)
    sum_x(2)
    grad_ring(4)
    sum_y(3)
    grad_end()
    sum_x(3)
    spread(1)
    for part_no in (0, 1):
        gather_beside("g", grad_slot, part_no)
    spread_on(1)
    collect(0)
    gather_steps("g", grad_slot, 1)
    gather_steps("g", grad_slot, 2)
    gather_steps("g", grad_slot, 3)
    gather_steps("g", grad_slot, 4)
    collect(1)
    out_act = pltpu.make_async_copy(rot, act_out, local_sem.at[0])
    out_act.start()
    for zoff in (0, 1, -1, 2, -2, 3, -3, 4):
        gather_sibling("g", grad_slot, zoff)
    out_grad = pltpu.make_async_copy(grot, grad_out, local_sem.at[1])
    out_grad.start()
    for one in sent:
        one.wait_send()
    out_act.wait()
    out_grad.wait()


def tiles(act_ref, grad_ref, out_ref):
    total = None
    for seq in range(2):
        left = act_ref[4 * seq : 4 * seq + 4].reshape(384, act_ref.shape[2])
        right = jnp.concatenate(
            [grad_ref[2 * seq : 2 * seq + 2, zc].reshape(384, 128) for zc in range(2)], axis=1
        )
        tile = lax.dot_general(left, right, (((0,), (0,)), ((), ())), preferred_element_type=F32)
        total = tile * tile if total is None else total + tile * tile
    out_ref[...] = total * F32(0.5)


def on_device(activations, out_grads, in_basis, out_basis):
    rows, depth = activations.shape
    wide = in_basis.shape[1]
    vmem = pl.BlockSpec(memory_space=pltpu.VMEM)
    hbm = pl.BlockSpec(memory_space=pl.ANY)
    act_rotated, grad_rotated = pl.pallas_call(
        exchange,
        out_shape=(
            jax.ShapeDtypeStruct((NZ, 96, wide), BF16),
            jax.ShapeDtypeStruct((4, NZ, 192, 128), BF16),
        ),
        in_specs=[vmem, vmem, hbm, hbm],
        out_specs=(hbm, hbm),
        scratch_shapes=[
            pltpu.VMEM(in_basis.shape, BF16),
            pltpu.VMEM(out_basis.shape, BF16),
            pltpu.VMEM((4, rows, depth // 2), F32),
            pltpu.VMEM((2, 2, NZ, 2, 48, depth // 4), BF16),
            pltpu.VMEM((4, 48, wide), F32),
            pltpu.VMEM((4, 3, 48, wide), BF16),
            pltpu.VMEM((4, 3, 48, wide), BF16),
            pltpu.VMEM((4, 48, wide), F32),
            pltpu.VMEM((4, 2, 24, wide), F32),
            pltpu.VMEM((4, 24, wide), F32),
            pltpu.VMEM((2, 48, wide), F32),
            pltpu.VMEM((2, NY, 2, 48, wide), BF16),
            pltpu.VMEM((NZ, 96, wide), BF16),
            pltpu.VMEM((8, 96, 256), BF16),
            pltpu.VMEM((2, NZ, 192, 128), F32),
            pltpu.VMEM((2, NZ, 192, 128), F32),
            pltpu.VMEM((2, NZ, 192, 128), F32),
            pltpu.VMEM((NZ, 192, 128), BF16),
            pltpu.VMEM((NZ, 192, 128), BF16),
            pltpu.VMEM((NZ, 192, 128), F32),
            pltpu.VMEM((2, 2, 4, 96, 128), F32),
            pltpu.VMEM((2, 2, 4, 96, 128), F32),
            pltpu.VMEM((4, NZ, 192, 128), BF16),
            pltpu.SemaphoreType.DMA((COPIES,)),
            pltpu.SemaphoreType.DMA((COPIES,)),
            pltpu.SemaphoreType.DMA((2,)),
        ],
        compiler_params=pltpu.CompilerParams(
            collective_id=0, has_side_effects=True, vmem_limit_bytes=VMEM_LIMIT
        ),
    )(activations, out_grads, in_basis, out_basis)
    return pl.pallas_call(
        tiles,
        grid=(4,),
        out_shape=jax.ShapeDtypeStruct((wide, 1024), F32),
        in_specs=[
            pl.BlockSpec((NZ, 96, wide), lambda i: (0, 0, 0)),
            pl.BlockSpec((4, 2, 192, 128), lambda i: (0, i, 0, 0)),
        ],
        out_specs=pl.BlockSpec((wide, 256), lambda i: (0, i)),
        compiler_params=pltpu.CompilerParams(vmem_limit_bytes=VMEM_LIMIT),
    )(act_rotated, grad_rotated)


def solution(mesh):
    placed = (P("row", "col"), P("col", "row"), P("col", "row"), P("row", "col"))
    return jax.shard_map(
        on_device, mesh=mesh, in_specs=placed, out_specs=P("row", "col"), check_vma=False
    )
```

```python
import functools

import jax
import jax.numpy as jnp
from jax import lax
from jax.experimental import pallas as pl
from jax.experimental.pallas import tpu as pltpu
from jax.sharding import PartitionSpec as P

MESH = pl.DeviceIdType.MESH
F32 = jnp.float32
BF16 = jnp.bfloat16
NZ, NY = 8, 4
COPIES = 264
VMEM_LIMIT = 58 * 2**20
FAR = (4, 3, -3, 2, -2, 1, -1, 0)
CHUNKS = ((0,), (1, -1), (2, -2), (3, -3), (4,))
SLOT = (0, 0, 1, 2, 1)
DIRECT = (False, False, False, False, True)
ORDER = (
    "pair", "ga", "a0", "gb", "ax", "a10", "a11", "gp", "basis", "c0", "a20", "gx", "c1", "a21", "gs0", "r0", "a30", "gs1",
    "r1", "c2", "y0", "gs2", "r2", "a31", "t0", "y1", "ge", "a40", "gy", "a41", "c3", "h10", "t1", "c4", "h11", "y2",
    "h20", "t2", "h21", "y3", "h30", "y4", "h31", "t3", "h40", "h41", "t4", "u0", "u1", "u2", "u3", "u4", "gf",
)


def ring(value, size):
    return lax.rem(value + size, size)


def exchange(
    act_ref, grad_ref, in_basis, out_basis, act_out, grad_out,
    basis, obasis, pair, acts, part, send_y, recv_y, own_y, rot_raw,
    thin, thin_send, thin_recv, thin_own, thin_raw, rot,
    grads, gsend, grecv, gown, gx_send, gx_recv, gsum, ring_send, ring_recv, grot,
    send_sem, recv_sem, local_sem,
):
    row, col = lax.axis_index("row"), lax.axis_index("col")
    z, xl, core = row // 4, lax.rem(row // 2, 2), lax.rem(row, 2)
    y, xh = col // 2, lax.rem(col, 2)

    def at(z=z, xl=xl, core=core, y=y, xh=xh):
        return (z * 4 + xl * 2 + core, y * 2 + xh)

    sibling, beside, across = at(core=1 - core), at(xl=1 - xl), at(xh=1 - xh)
    up = (at(z=ring(z + 1, NZ)), at(z=ring(z - 1, NZ)))
    around = [at(y=ring(y + rel, NY)) for rel in (1, 2, 3)]
    members = [(rel, side) for rel in range(NY) for side in (0, 1)][1:]
    member = {(rel, side): at(y=ring(y + rel, NY), xh=1 - xh if side else xh) for rel, side in members}
    ids, sent, stored = {}, [], []

    def place(zoff):
        return ring(z + zoff, NZ)


    def copy(key, src, dst, device):
        number = ids.setdefault(key, len(ids))
        return pltpu.make_async_remote_copy(
            src_ref=src, dst_ref=dst, send_sem=send_sem.at[number], recv_sem=recv_sem.at[number],
            device_id=device, device_id_type=MESH,
        )

    def send(key, src, dst, device):
        one = copy(key, src, dst, device)
        one.start()
        sent.append(one)

    def arrive(key, dst):
        copy(key, dst, dst, sibling).wait_recv()

    load_basis = pltpu.make_async_copy(in_basis, basis, local_sem.at[8])
    load_obasis = pltpu.make_async_copy(out_basis, obasis, local_sem.at[9])
    load_obasis.start()
    load_basis.start()

    barrier = pltpu.get_barrier_semaphore()
    near = [sibling, beside, *(at(z=place(zoff)) for zoff in FAR[:-1]), *member.values()]
    for device in near:
        pl.semaphore_signal(barrier, inc=1, device_id=device, device_id_type=MESH)
    half = act_ref.shape[1] // 2
    quarter = half // 2
    mine = act_ref[...].astype(F32)
    for number in range(2):
        pair[2 + number] = mine[:, number * half : (number + 1) * half]
    pair[core] = pair[2 + core]
    grads[col] = grad_ref[...]
    pl.semaphore_wait(barrier, len(near))

    def act_slot(zz, q, part_no, side=0):
        kk = core if side == 0 else 1 - core
        return acts.at[kk, part_no, zz, xl if q == 0 else 1 - xl]

    def grad_slot(zz, q, part_no, side=0):
        kk = core if side == 0 else 1 - core
        return grot.at[2 * kk + (xl if q == 0 else 1 - xl), zz, pl.ds(96 * part_no, 96)]

    def gather_put(name, slot, q, part_no):
        ref = slot(z, q, part_no)
        for way in (0, 1):
            send((name, way, 1, q, part_no), ref, ref, up[way])
        if q == 0:
            send((name, "x", part_no), ref, ref, beside)
        send((name, "sib", 0, q, part_no), ref, ref, sibling)

    def gather_beside(name, slot, part_no):
        arrive((name, "x", part_no), slot(z, 1, part_no))
        gather_put(name, slot, 1, part_no)

    def gather_step(name, slot, step, way, q, part_no):
        if step == 4 and part_no != way:
            return
        zoff = 4 if step == 4 else (-step if way == 0 else step)
        ref = slot(place(zoff), q, part_no)
        arrive((name, way, step, q, part_no), ref)
        if step < 3 or (step == 3 and part_no == way):
            send((name, way, step + 1, q, part_no), ref, ref, up[way])
        send((name, "sib", zoff, q, part_no), ref, ref, sibling)

    def gather_steps(name, slot, step, q):
        for part_no in (0, 1):
            for way in (0, 1):
                gather_step(name, slot, step, way, q, part_no)

    def gather_sibling(name, slot, zoff):
        for q in (0, 1):
            for part_no in (0, 1):
                arrive((name, "sib", zoff, q, part_no), slot(place(zoff), q, part_no, 1))

    def partial(seq, ref):
        got = jnp.dot(grads[pl.ds(4 * seq, 4)].reshape(384, 256), obasis[...], preferred_element_type=F32)
        for side in range(2):
            for zc in range(NZ):
                ref[side, zc] = got[192 * side : 192 * side + 192, 128 * zc : 128 * zc + 128]

    def rotate(zoffs):
        for zoff in zoffs:
            gather_sibling("a", act_slot, zoff)
        left = jnp.concatenate(
            [
                jnp.concatenate([acts[kk, pp, place(zoff)].reshape(96, quarter) for zoff in zoffs], axis=0)
                for kk in (0, 1)
                for pp in (0, 1)
            ],
            axis=1,
        )
        return jnp.dot(left, basis[...], preferred_element_type=F32)

    def piece_of(wide, yy, hh):
        return (hh, yy) if wide else (2 * lax.rem(yy, 2) + hh, yy // 2)

    def chunk(j):
        zoffs, wide = CHUNKS[j], len(CHUNKS[j]) == 2
        got = rotate(zoffs)
        if wide:
            for n, at_col in enumerate((0, 384)):
                part[n] = got[:, at_col : at_col + 512].reshape(4, 48, 512)
        else:
            for n, at_col in enumerate((0, 256, 512, 640)):
                thin[n] = got[:, at_col : at_col + 256].reshape(2, 48, 256)
        parts, out, came, own = (part, send_y, recv_y, own_y) if wide else (thin, thin_send, thin_recv, thin_own)
        i = SLOT[j]
        for n, (rel, side) in enumerate(members):
            a, b = piece_of(wide, ring(y + rel, NY), 1 - xh if side else xh)
            out[i, n] = parts[a, b].astype(BF16)
            send(("s2", j, n), out.at[i, n], came.at[i, n], member[rel, side])
        a, b = piece_of(wide, y, xh)
        own[i] = parts[a, b]

    def sum_up(j):
        wide, i = len(CHUNKS[j]) == 2, SLOT[j]
        came, own, raw = (recv_y, own_y, rot_raw) if wide else (thin_recv, thin_own, thin_raw)
        total = own[i]
        for n in range(7):
            arrive(("s2", j, n), came.at[i, n])
            total = total + came[i, n].astype(F32)
        raw[i, y, xh] = total.astype(BF16)
        ref = raw.at[i, y, xh]
        if DIRECT[j]:
            for rel, side in members:
                send(("s3", j, rel, side), ref, ref, member[rel, side])
        else:
            send(("s3", j, 0, 1), ref, ref, across)
            for rel in (1, 2, 3):
                send(("s3", j, rel, 0), ref, ref, around[rel - 1])

    def spread_on(j):
        raw = rot_raw if len(CHUNKS[j]) == 2 else thin_raw
        ref = raw.at[SLOT[j], y, 1 - xh]
        arrive(("s3", j, 0, 1), ref)
        if not DIRECT[j]:
            for rel in (1, 2, 3):
                send(("s3", j, rel, 1), ref, ref, around[rel - 1])

    def collect(j):
        zoffs, i = CHUNKS[j], SLOT[j]
        wide = len(zoffs) == 2
        raw = rot_raw if wide else thin_raw
        for rel in (1, 2, 3):
            for side in (0, 1):
                arrive(("s3", j, rel, side), raw.at[i, ring(y - rel, NY), 1 - xh if side else xh])
        if wide:
            whole = jnp.concatenate([raw[i, :, 0], raw[i, :, 1][:, :, 128:]], axis=2)
        else:
            halves = [
                jnp.concatenate(
                    [raw[i, 2 * n, 0], raw[i, 2 * n, 1], raw[i, 2 * n + 1, 0], raw[i, 2 * n + 1, 1][:, 128:]], axis=1
                )
                for n in (0, 1)
            ]
        for n, zoff in enumerate(zoffs):
            zz = place(zoff)
            if wide:
                rot[zz] = whole[2 * n : 2 * n + 2].reshape(96, -1)
            else:
                rot[zz] = jnp.concatenate(halves, axis=0)
            one = pltpu.make_async_copy(rot.at[zz], act_out.at[zz], local_sem.at[zoff + 3])
            one.start()
            stored.append(one)

    def grad_beside():
        arrive(("g2core", 0), grecv.at[1 - xl])
        for zoff in FAR:
            zc = place(zoff)
            gx_send[zc] = (gown[1 - xl, zc] + grecv[1 - xl, zc]).astype(BF16)
            send(("g2x", zoff), gx_send.at[zc], gx_recv.at[zc], beside)
        arrive(("g2core", 1), grecv.at[xl])

    def grad_sum(offsets):
        for zoff in offsets:
            zc = place(zoff)
            arrive(("g2x", zoff), gx_recv.at[zc])
            gsum[zc] = gown[xl, zc] + grecv[xl, zc] + gx_recv[zc].astype(F32)

    def grad_spread(offsets):
        for zoff in offsets:
            n = zoff + 3
            ring_send[n] = gsum[place(zoff)].astype(BF16)
            send(("g2", zoff), ring_send.at[n], ring_recv.at[n], at(z=place(zoff)))

    def grad_end():
        value = gsum[z]
        for zoff in FAR[:-1]:
            arrive(("g2", zoff), ring_recv.at[zoff + 3])
            value = value + ring_recv[zoff + 3].astype(F32)
        grot[2 * core + xl, z] = value.astype(BF16)
        for part_no in (0, 1):
            gather_put("g", grad_slot, 0, part_no)

    def act_pair():
        send("pair", pair.at[3 - core], pair.at[core], sibling)

    def act_start():
        arrive("pair", pair.at[1 - core])
        block = pair[0:2].reshape(48, half).astype(BF16)
        for part_no in (0, 1):
            acts[core, part_no, z, xl] = block[:, part_no * quarter : (part_no + 1) * quarter]
        for part_no in (0, 1):
            gather_put("a", act_slot, 0, part_no)

    def act_beside():
        for part_no in (0, 1):
            gather_beside("a", act_slot, part_no)

    def grad_start():
        send(("g1", 0), grads.at[col], grads.at[col], across)
        for rel in (1, 2, 3):
            send(("g1", rel, 0), grads.at[col], grads.at[col], around[rel - 1])

    def grad_on():
        other = y * 2 + 1 - xh
        arrive(("g1", 0), grads.at[other])
        for rel in (1, 2, 3):
            send(("g1", rel, 1), grads.at[other], grads.at[other], around[rel - 1])

    def grad_partial():
        for rel in (1, 2, 3):
            came = ring(y - rel, NY) * 2
            arrive(("g1", rel, 0), grads.at[came + xh])
            arrive(("g1", rel, 1), grads.at[came + 1 - xh])
        load_obasis.wait()
        partial(1 - core, gsend)
        for n, side in enumerate((1 - xl, xl)):
            send(("g2core", n), gsend.at[side], grecv.at[side], sibling)
        partial(core, gown)

    def grad_gather_start():
        for part_no in (0, 1):
            gather_beside("g", grad_slot, part_no)

    out_grad = pltpu.make_async_copy(grot, grad_out, local_sem.at[10])

    def grad_finish():
        for zoff in (0, 1, -1, 2, -2, 3, -3, 4):
            gather_sibling("g", grad_slot, zoff)
        out_grad.start()

    def act_siblings():
        for zoff in (0, 1, -1, 2, -2, 3, -3, 4):
            gather_sibling("a", act_slot, zoff)

    steps = {
        "pair": act_pair, "ga": grad_start, "a0": act_start, "gb": grad_on, "ax": act_beside, "gp": grad_partial,
        "gx": grad_beside, "ge": grad_end, "gy": grad_gather_start, "gf": grad_finish,
        "basis": load_basis.wait, "ob": load_obasis.wait, "asib": act_siblings, "og": out_grad.start,
    }
    for n, offsets in enumerate((FAR[:3], FAR[3:5], FAR[5:])):
        steps[f"gs{n}"] = functools.partial(grad_sum, offsets)
    for n in range(4):
        for q in (0, 1):
            steps[f"a{n + 1}{q}"] = functools.partial(gather_steps, "a", act_slot, n + 1, q)
            steps[f"h{n + 1}{q}"] = functools.partial(gather_steps, "g", grad_slot, n + 1, q)
    for n, offsets in enumerate((FAR[:3], FAR[3:5], FAR[5:7])):
        steps[f"r{n}"] = functools.partial(grad_spread, offsets)
    for n in range(5):
        steps[f"c{n}"] = functools.partial(chunk, n)
        steps[f"y{n}"] = functools.partial(sum_up, n)
        steps[f"t{n}"] = functools.partial(spread_on, n)
        steps[f"u{n}"] = functools.partial(collect, n)
    for name in ORDER:
        steps[name]()
    for one in sent:
        one.wait_send()
    for one in stored:
        one.wait()
    out_grad.wait()


def tiles(act_hbm, grad_hbm, out_hbm, act, grad, turned, out, in_sem, out_sem):
    wide = act.shape[2]
    loads = []
    for seq in range(2):
        for n, (src, dst, step) in enumerate(((act_hbm, act, 4), (grad_hbm, grad, 2))):
            rows = pl.ds(step * seq, step)
            loads.append(pltpu.make_async_copy(src.at[rows], dst.at[rows], in_sem.at[2 * seq + n]))
    for one in loads:
        one.start()
    stores = []
    for seq in range(2):
        loads[2 * seq].wait()
        turned[seq] = act[4 * seq : 4 * seq + 4].reshape(384, wide).T
        loads[2 * seq + 1].wait()
    for n in range(4):
        total = None
        for seq in range(2):
            right = jnp.concatenate(
                [grad[2 * seq : 2 * seq + 2, 2 * n + zc].reshape(384, 128) for zc in range(2)], axis=1
            )
            tile = jnp.dot(turned[seq], right, preferred_element_type=F32)
            total = tile * tile if total is None else total + tile * tile
        out[n] = total * F32(0.5)
        one = pltpu.make_async_copy(out.at[n], out_hbm.at[:, pl.ds(256 * n, 256)], out_sem.at[n])
        one.start()
        stores.append(one)
    for one in stores:
        one.wait()


def on_device(activations, out_grads, in_basis, out_basis):
    rows, depth = activations.shape
    wide = in_basis.shape[1]
    vmem = pl.BlockSpec(memory_space=pltpu.VMEM)
    hbm = pl.BlockSpec(memory_space=pl.ANY)
    act_rotated, grad_rotated = pl.pallas_call(
        exchange,
        out_shape=(
            jax.ShapeDtypeStruct((NZ, 96, wide), BF16),
            jax.ShapeDtypeStruct((4, NZ, 192, 128), BF16),
        ),
        in_specs=[vmem, vmem, hbm, hbm],
        out_specs=(hbm, hbm),
        scratch_shapes=[
            pltpu.VMEM(in_basis.shape, BF16),
            pltpu.VMEM(out_basis.shape, BF16),
            pltpu.VMEM((4, rows, depth // 2), F32),
            pltpu.VMEM((2, 2, NZ, 2, 48, depth // 4), BF16),
            pltpu.VMEM((2, NY, 48, 512), F32),
            pltpu.VMEM((3, 7, 48, 512), BF16),
            pltpu.VMEM((3, 7, 48, 512), BF16),
            pltpu.VMEM((3, 48, 512), F32),
            pltpu.VMEM((3, NY, 2, 48, 512), BF16),
            pltpu.VMEM((4, 2, 48, 256), F32),
            pltpu.VMEM((2, 7, 48, 256), BF16),
            pltpu.VMEM((2, 7, 48, 256), BF16),
            pltpu.VMEM((2, 48, 256), F32),
            pltpu.VMEM((2, NY, 2, 48, 256), BF16),
            pltpu.VMEM((NZ, 96, wide), BF16),
            pltpu.VMEM((8, 96, 256), BF16),
            pltpu.VMEM((2, NZ, 192, 128), F32),
            pltpu.VMEM((2, NZ, 192, 128), F32),
            pltpu.VMEM((2, NZ, 192, 128), F32),
            pltpu.VMEM((NZ, 192, 128), BF16),
            pltpu.VMEM((NZ, 192, 128), BF16),
            pltpu.VMEM((NZ, 192, 128), F32),
            pltpu.VMEM((NZ, 192, 128), BF16),
            pltpu.VMEM((NZ, 192, 128), BF16),
            pltpu.VMEM((4, NZ, 192, 128), BF16),
            pltpu.SemaphoreType.DMA((COPIES,)),
            pltpu.SemaphoreType.DMA((COPIES,)),
            pltpu.SemaphoreType.DMA((11,)),
        ],
        compiler_params=pltpu.CompilerParams(
            collective_id=0, has_side_effects=True, vmem_limit_bytes=VMEM_LIMIT
        ),
    )(activations, out_grads, in_basis, out_basis)
    return pl.pallas_call(
        tiles,
        out_shape=jax.ShapeDtypeStruct((wide, 1024), F32),
        in_specs=[hbm, hbm],
        out_specs=hbm,
        scratch_shapes=[
            pltpu.VMEM((NZ, 96, wide), BF16),
            pltpu.VMEM((4, NZ, 192, 128), BF16),
            pltpu.VMEM((2, wide, 384), BF16),
            pltpu.VMEM((4, wide, 256), F32),
            pltpu.SemaphoreType.DMA((4,)),
            pltpu.SemaphoreType.DMA((4,)),
        ],
        compiler_params=pltpu.CompilerParams(vmem_limit_bytes=VMEM_LIMIT),
    )(act_rotated, grad_rotated)


def solution(mesh):
    placed = (P("row", "col"), P("col", "row"), P("col", "row"), P("row", "col"))
    return jax.shard_map(
        on_device, mesh=mesh, in_specs=placed, out_specs=P("row", "col"), check_vma=False
    )
```

```python
import functools

import jax
import jax.numpy as jnp
from jax import lax
from jax.experimental import pallas as pl
from jax.experimental.pallas import tpu as pltpu
from jax.sharding import PartitionSpec as P

MESH = pl.DeviceIdType.MESH
F32 = jnp.float32
BF16 = jnp.bfloat16
NZ, NY = 8, 4
COPIES = 264
VMEM_LIMIT = 58 * 2**20
FAR = (4, 3, -3, 2, -2, 1, -1, 0)
CHUNKS = ((0,), (1, -1), (2, -2), (3, -3), (4,))
SLOT = (0, 0, 1, 2, 1)
FIRST = {"a": (1,), "g": (1, 2)}
ONWARD = {"a": {1: (2,), 2: (3,), 3: (4,)}, "g": {2: (3, 4)}}
DIRECT = (False, False, False, False, True)
ORDER = (
    "pair", "ga", "a0", "gb", "ax", "a10", "a11", "gp", "basis", "c0", "a20", "gx", "c1", "a21", "y0", "gs0", "r0", "a30",
    "gs1", "r1", "c2", "t0", "gs2", "r2", "a31", "c3", "y1", "a40", "a41", "c4", "f0", "ge", "gy", "t1", "y2", "h20",
    "f1", "h21", "t2", "h10", "h11", "y3", "h30", "f2", "y4", "h31", "t3", "k0", "u0", "k1", "u1", "h40", "h41", "t4",
    "f3", "k2", "u2", "k3", "u3", "u4", "k4",
)


def ring(value, size):
    return lax.rem(value + size, size)


def exchange(
    act_ref, grad_ref, in_basis, out_basis, act_out, grad_out,
    basis, obasis, pair, acts, part, send_y, recv_y, own_y, rot_raw,
    thin, thin_send, thin_recv, thin_own, thin_raw, rot,
    grads, gsend, grecv, gown, gx_send, gx_recv, gsum, ring_send, ring_recv, grot,
    send_sem, recv_sem, local_sem,
):
    row, col = lax.axis_index("row"), lax.axis_index("col")
    z, xl, core = row // 4, lax.rem(row // 2, 2), lax.rem(row, 2)
    y, xh = col // 2, lax.rem(col, 2)

    def at(z=z, xl=xl, core=core, y=y, xh=xh):
        return (z * 4 + xl * 2 + core, y * 2 + xh)

    sibling, beside, across = at(core=1 - core), at(xl=1 - xl), at(xh=1 - xh)
    around = [at(y=ring(y + rel, NY)) for rel in (1, 2, 3)]
    members = [(rel, side) for rel in range(NY) for side in (0, 1)][1:]
    member = {(rel, side): at(y=ring(y + rel, NY), xh=1 - xh if side else xh) for rel, side in members}
    ids, sent, stored = {}, [], []

    def place(zoff):
        return ring(z + zoff, NZ)


    def copy(key, src, dst, device):
        number = ids.setdefault(key, len(ids))
        return pltpu.make_async_remote_copy(
            src_ref=src, dst_ref=dst, send_sem=send_sem.at[number], recv_sem=recv_sem.at[number],
            device_id=device, device_id_type=MESH,
        )

    def send(key, src, dst, device):
        one = copy(key, src, dst, device)
        one.start()
        sent.append(one)

    def arrive(key, dst):
        copy(key, dst, dst, sibling).wait_recv()

    load_basis = pltpu.make_async_copy(in_basis, basis, local_sem.at[8])
    load_obasis = pltpu.make_async_copy(out_basis, obasis, local_sem.at[9])
    load_obasis.start()
    load_basis.start()

    barrier = pltpu.get_barrier_semaphore()
    near = [sibling, beside, *(at(z=place(zoff)) for zoff in FAR[:-1]), *member.values()]
    for device in near:
        pl.semaphore_signal(barrier, inc=1, device_id=device, device_id_type=MESH)
    half = act_ref.shape[1] // 2
    quarter = half // 2
    mine = act_ref[...].astype(F32)
    for number in range(2):
        pair[2 + number] = mine[:, number * half : (number + 1) * half]
    pair[core] = pair[2 + core]
    grads[col] = grad_ref[...]
    pl.semaphore_wait(barrier, len(near))

    def act_slot(zz, q, part_no, side=0):
        kk = core if side == 0 else 1 - core
        return acts.at[kk, part_no, zz, xl if q == 0 else 1 - xl]

    def grad_slot(zz, q, part_no, side=0):
        kk = core if side == 0 else 1 - core
        return grot.at[2 * kk + (xl if q == 0 else 1 - xl), zz, pl.ds(96 * part_no, 96)]

    def along(way, hops):
        return at(z=place(hops if way == 0 else -hops))

    def gather_put(name, slot, q, part_no):
        ref = slot(z, q, part_no)
        for way in (0, 1):
            for step in FIRST[name]:
                send((name, way, step, q, part_no), ref, ref, along(way, step))
        if q == 0:
            send((name, "x", part_no), ref, ref, beside)
        send((name, "sib", 0, q, part_no), ref, ref, sibling)

    def gather_beside(name, slot, part_no):
        arrive((name, "x", part_no), slot(z, 1, part_no))
        gather_put(name, slot, 1, part_no)

    def gather_step(name, slot, step, way, q, part_no):
        if step == 4 and part_no != way:
            return
        zoff = 4 if step == 4 else (-step if way == 0 else step)
        ref = slot(place(zoff), q, part_no)
        arrive((name, way, step, q, part_no), ref)
        for later in ONWARD[name].get(step, ()):
            if later < 4 or part_no == way:
                send((name, way, later, q, part_no), ref, ref, along(way, later - step))
        send((name, "sib", zoff, q, part_no), ref, ref, sibling)

    def gather_steps(name, slot, step, q):
        for part_no in (0, 1):
            for way in (0, 1):
                gather_step(name, slot, step, way, q, part_no)

    def gather_sibling(name, slot, zoff):
        for q in (0, 1):
            for part_no in (0, 1):
                arrive((name, "sib", zoff, q, part_no), slot(place(zoff), q, part_no, 1))

    def partial(seq, ref):
        got = jnp.dot(grads[pl.ds(4 * seq, 4)].reshape(384, 256), obasis[...], preferred_element_type=F32)
        for side in range(2):
            for zc in range(NZ):
                ref[side, zc] = got[192 * side : 192 * side + 192, 128 * zc : 128 * zc + 128]

    def rotate(zoffs):
        for zoff in zoffs:
            gather_sibling("a", act_slot, zoff)
        left = jnp.concatenate(
            [
                jnp.concatenate([acts[kk, pp, place(zoff)].reshape(96, quarter) for zoff in zoffs], axis=0)
                for kk in (0, 1)
                for pp in (0, 1)
            ],
            axis=1,
        )
        return jnp.dot(left, basis[...], preferred_element_type=F32)

    def piece_of(wide, yy, hh):
        return (hh, yy) if wide else (2 * lax.rem(yy, 2) + hh, yy // 2)

    def chunk(j):
        zoffs, wide = CHUNKS[j], len(CHUNKS[j]) == 2
        got = rotate(zoffs)
        if wide:
            for n, at_col in enumerate((0, 384)):
                part[n] = got[:, at_col : at_col + 512].reshape(4, 48, 512)
        else:
            for n, at_col in enumerate((0, 256, 512, 640)):
                thin[n] = got[:, at_col : at_col + 256].reshape(2, 48, 256)
        parts, out, came, own = (part, send_y, recv_y, own_y) if wide else (thin, thin_send, thin_recv, thin_own)
        i = SLOT[j]
        for n, (rel, side) in enumerate(members):
            a, b = piece_of(wide, ring(y + rel, NY), 1 - xh if side else xh)
            out[i, n] = parts[a, b].astype(BF16)
            send(("s2", j, n), out.at[i, n], came.at[i, n], member[rel, side])
        a, b = piece_of(wide, y, xh)
        own[i] = parts[a, b]

    def sum_up(j):
        wide, i = len(CHUNKS[j]) == 2, SLOT[j]
        came, own, raw = (recv_y, own_y, rot_raw) if wide else (thin_recv, thin_own, thin_raw)
        total = own[i]
        for n in range(7):
            arrive(("s2", j, n), came.at[i, n])
            total = total + came[i, n].astype(F32)
        raw[i, y, xh] = total.astype(BF16)
        ref = raw.at[i, y, xh]
        if DIRECT[j]:
            for rel, side in members:
                send(("s3", j, rel, side), ref, ref, member[rel, side])
        else:
            send(("s3", j, 0, 1), ref, ref, across)
            for rel in (1, 2, 3):
                send(("s3", j, rel, 0), ref, ref, around[rel - 1])

    def spread_on(j):
        raw = rot_raw if len(CHUNKS[j]) == 2 else thin_raw
        ref = raw.at[SLOT[j], y, 1 - xh]
        arrive(("s3", j, 0, 1), ref)
        if not DIRECT[j]:
            for rel in (1, 2, 3):
                send(("s3", j, rel, 1), ref, ref, around[rel - 1])

    def collect(j):
        zoffs, i = CHUNKS[j], SLOT[j]
        wide = len(zoffs) == 2
        raw = rot_raw if wide else thin_raw
        for rel in (1, 2, 3):
            for side in (0, 1):
                arrive(("s3", j, rel, side), raw.at[i, ring(y - rel, NY), 1 - xh if side else xh])
        if wide:
            whole = jnp.concatenate([raw[i, :, 0], raw[i, :, 1][:, :, 128:]], axis=2)
        else:
            halves = [
                jnp.concatenate(
                    [raw[i, 2 * n, 0], raw[i, 2 * n, 1], raw[i, 2 * n + 1, 0], raw[i, 2 * n + 1, 1][:, 128:]], axis=1
                )
                for n in (0, 1)
            ]
        for n, zoff in enumerate(zoffs):
            zz = place(zoff)
            if wide:
                rot[zz] = whole[2 * n : 2 * n + 2].reshape(96, -1)
            else:
                rot[zz] = jnp.concatenate(halves, axis=0)
            one = pltpu.make_async_copy(rot.at[zz], act_out.at[zz], local_sem.at[zoff + 3])
            one.start()
            stored.append(one)

    def grad_beside():
        arrive(("g2core", 0), grecv.at[1 - xl])
        for zoff in FAR:
            zc = place(zoff)
            gx_send[zc] = (gown[1 - xl, zc] + grecv[1 - xl, zc]).astype(BF16)
            send(("g2x", zoff), gx_send.at[zc], gx_recv.at[zc], beside)
        arrive(("g2core", 1), grecv.at[xl])

    def grad_sum(offsets):
        for zoff in offsets:
            zc = place(zoff)
            arrive(("g2x", zoff), gx_recv.at[zc])
            gsum[zc] = gown[xl, zc] + grecv[xl, zc] + gx_recv[zc].astype(F32)

    def grad_spread(offsets):
        for zoff in offsets:
            n = zoff + 3
            ring_send[n] = gsum[place(zoff)].astype(BF16)
            send(("g2", zoff), ring_send.at[n], ring_recv.at[n], at(z=place(zoff)))

    def grad_end():
        value = gsum[z]
        for zoff in FAR[:-1]:
            arrive(("g2", zoff), ring_recv.at[zoff + 3])
            value = value + ring_recv[zoff + 3].astype(F32)
        grot[2 * core + xl, z] = value.astype(BF16)
        for part_no in (0, 1):
            gather_put("g", grad_slot, 0, part_no)

    def act_pair():
        send("pair", pair.at[3 - core], pair.at[core], sibling)

    def act_start():
        arrive("pair", pair.at[1 - core])
        block = pair[0:2].reshape(48, half).astype(BF16)
        for part_no in (0, 1):
            acts[core, part_no, z, xl] = block[:, part_no * quarter : (part_no + 1) * quarter]
        for part_no in (0, 1):
            gather_put("a", act_slot, 0, part_no)

    def act_beside():
        for part_no in (0, 1):
            gather_beside("a", act_slot, part_no)

    def grad_start():
        send(("g1", 0), grads.at[col], grads.at[col], across)
        for rel in (1, 2, 3):
            send(("g1", rel, 0), grads.at[col], grads.at[col], around[rel - 1])

    def grad_on():
        other = y * 2 + 1 - xh
        arrive(("g1", 0), grads.at[other])
        for rel in (1, 2, 3):
            send(("g1", rel, 1), grads.at[other], grads.at[other], around[rel - 1])

    def grad_partial():
        for rel in (1, 2, 3):
            came = ring(y - rel, NY) * 2
            arrive(("g1", rel, 0), grads.at[came + xh])
            arrive(("g1", rel, 1), grads.at[came + 1 - xh])
        load_obasis.wait()
        partial(1 - core, gsend)
        for n, side in enumerate((1 - xl, xl)):
            send(("g2core", n), gsend.at[side], grecv.at[side], sibling)
        partial(core, gown)

    def grad_gather_start():
        for part_no in (0, 1):
            gather_beside("g", grad_slot, part_no)

    def grad_store(offsets):
        for zoff in offsets:
            gather_sibling("g", grad_slot, zoff)
            zz = place(zoff)
            one = pltpu.make_async_copy(grot.at[:, zz], grad_out.at[:, zz], local_sem.at[zoff + 13])
            one.start()
            stored.append(one)

    def flush():
        while len(sent) > 48:
            sent.pop(0).wait_send()

    steps = {
        "pair": act_pair, "ga": grad_start, "a0": act_start, "gb": grad_on, "ax": act_beside, "gp": grad_partial,
        "gx": grad_beside, "ge": grad_end, "gy": grad_gather_start,
        "basis": load_basis.wait, "f0": flush, "f1": flush, "f2": flush, "f3": flush,
    }
    for n, offsets in enumerate((FAR[:3], FAR[3:5], FAR[5:])):
        steps[f"gs{n}"] = functools.partial(grad_sum, offsets)
    for n in range(4):
        for q in (0, 1):
            steps[f"a{n + 1}{q}"] = functools.partial(gather_steps, "a", act_slot, n + 1, q)
            steps[f"h{n + 1}{q}"] = functools.partial(gather_steps, "g", grad_slot, n + 1, q)
    for n, offsets in enumerate(((0,), (1, -1), (2, -2), (3, -3), (4,))):
        steps[f"k{n}"] = functools.partial(grad_store, offsets)
    for n, offsets in enumerate((FAR[:3], FAR[3:5], FAR[5:7])):
        steps[f"r{n}"] = functools.partial(grad_spread, offsets)
    for n in range(5):
        steps[f"c{n}"] = functools.partial(chunk, n)
        steps[f"y{n}"] = functools.partial(sum_up, n)
        steps[f"t{n}"] = functools.partial(spread_on, n)
        steps[f"u{n}"] = functools.partial(collect, n)
    for name in ORDER:
        steps[name]()
    for one in sent:
        one.wait_send()
    for one in stored:
        one.wait()


def tiles(act_hbm, grad_hbm, out_hbm, act, grad, turned, out, in_sem, out_sem):
    wide = act.shape[2]
    loads = []
    for seq in range(2):
        for n, (src, dst, step) in enumerate(((act_hbm, act, 4), (grad_hbm, grad, 2))):
            rows = pl.ds(step * seq, step)
            loads.append(pltpu.make_async_copy(src.at[rows], dst.at[rows], in_sem.at[2 * seq + n]))
    for one in loads:
        one.start()
    stores = []
    for seq in range(2):
        loads[2 * seq].wait()
        turned[seq] = act[4 * seq : 4 * seq + 4].reshape(384, wide).T
        loads[2 * seq + 1].wait()
    for n in range(4):
        total = None
        for seq in range(2):
            right = jnp.concatenate(
                [grad[2 * seq : 2 * seq + 2, 2 * n + zc].reshape(384, 128) for zc in range(2)], axis=1
            )
            tile = jnp.dot(turned[seq], right, preferred_element_type=F32)
            total = tile * tile if total is None else total + tile * tile
        out[n] = total * F32(0.5)
        one = pltpu.make_async_copy(out.at[n], out_hbm.at[:, pl.ds(256 * n, 256)], out_sem.at[n])
        one.start()
        stores.append(one)
    for one in stores:
        one.wait()


def on_device(activations, out_grads, in_basis, out_basis):
    rows, depth = activations.shape
    wide = in_basis.shape[1]
    vmem = pl.BlockSpec(memory_space=pltpu.VMEM)
    hbm = pl.BlockSpec(memory_space=pl.ANY)
    act_rotated, grad_rotated = pl.pallas_call(
        exchange,
        out_shape=(
            jax.ShapeDtypeStruct((NZ, 96, wide), BF16),
            jax.ShapeDtypeStruct((4, NZ, 192, 128), BF16),
        ),
        in_specs=[vmem, vmem, hbm, hbm],
        out_specs=(hbm, hbm),
        scratch_shapes=[
            pltpu.VMEM(in_basis.shape, BF16),
            pltpu.VMEM(out_basis.shape, BF16),
            pltpu.VMEM((4, rows, depth // 2), F32),
            pltpu.VMEM((2, 2, NZ, 2, 48, depth // 4), BF16),
            pltpu.VMEM((2, NY, 48, 512), F32),
            pltpu.VMEM((3, 7, 48, 512), BF16),
            pltpu.VMEM((3, 7, 48, 512), BF16),
            pltpu.VMEM((3, 48, 512), F32),
            pltpu.VMEM((3, NY, 2, 48, 512), BF16),
            pltpu.VMEM((4, 2, 48, 256), F32),
            pltpu.VMEM((2, 7, 48, 256), BF16),
            pltpu.VMEM((2, 7, 48, 256), BF16),
            pltpu.VMEM((2, 48, 256), F32),
            pltpu.VMEM((2, NY, 2, 48, 256), BF16),
            pltpu.VMEM((NZ, 96, wide), BF16),
            pltpu.VMEM((8, 96, 256), BF16),
            pltpu.VMEM((2, NZ, 192, 128), F32),
            pltpu.VMEM((2, NZ, 192, 128), F32),
            pltpu.VMEM((2, NZ, 192, 128), F32),
            pltpu.VMEM((NZ, 192, 128), BF16),
            pltpu.VMEM((NZ, 192, 128), BF16),
            pltpu.VMEM((NZ, 192, 128), F32),
            pltpu.VMEM((NZ, 192, 128), BF16),
            pltpu.VMEM((NZ, 192, 128), BF16),
            pltpu.VMEM((4, NZ, 192, 128), BF16),
            pltpu.SemaphoreType.DMA((COPIES,)),
            pltpu.SemaphoreType.DMA((COPIES,)),
            pltpu.SemaphoreType.DMA((18,)),
        ],
        compiler_params=pltpu.CompilerParams(
            collective_id=0, has_side_effects=True, vmem_limit_bytes=VMEM_LIMIT
        ),
    )(activations, out_grads, in_basis, out_basis)
    return pl.pallas_call(
        tiles,
        out_shape=jax.ShapeDtypeStruct((wide, 1024), F32),
        in_specs=[hbm, hbm],
        out_specs=hbm,
        scratch_shapes=[
            pltpu.VMEM((NZ, 96, wide), BF16),
            pltpu.VMEM((4, NZ, 192, 128), BF16),
            pltpu.VMEM((2, wide, 384), BF16),
            pltpu.VMEM((4, wide, 256), F32),
            pltpu.SemaphoreType.DMA((4,)),
            pltpu.SemaphoreType.DMA((4,)),
        ],
        compiler_params=pltpu.CompilerParams(vmem_limit_bytes=VMEM_LIMIT),
    )(act_rotated, grad_rotated)


def solution(mesh):
    placed = (P("row", "col"), P("col", "row"), P("col", "row"), P("row", "col"))
    return jax.shard_map(
        on_device, mesh=mesh, in_specs=placed, out_specs=P("row", "col"), check_vma=False
    )
```

```python
import functools

import jax
import jax.numpy as jnp
from jax import lax
from jax.experimental import pallas as pl
from jax.experimental.pallas import tpu as pltpu
from jax.sharding import PartitionSpec as P

MESH = pl.DeviceIdType.MESH
F32 = jnp.float32
BF16 = jnp.bfloat16
NZ, NY = 8, 4
COPIES = 264
VMEM_LIMIT = 58 * 2**20
FAR = (4, 3, -3, 2, -2, 1, -1, 0)
CHUNKS = ((0,), (1, -1), (2, -2), (3, -3), (4,))
SLOT = (0, 0, 1, 2, 1)
FIRST = {"a": (1,), "g": (1, 2)}
ONWARD = {"a": {1: (2,), 2: (3,), 3: (4,)}, "g": {2: (3, 4)}}
DIRECT = (False, False, False, False, True)
ORDER = (
    "pair", "ga", "a0", "gb", "ax", "a10", "a11", "gp", "basis", "c0", "a20", "gx", "c1", "a21", "y0", "gs0", "r0", "a30",
    "gs1", "r1", "c2", "t0", "gs2", "r2", "a31", "c3", "y1", "a40", "a41", "c4", "f0", "ge", "gy", "t1", "y2", "h20",
    "f1", "h21", "t2", "h10", "h11", "y3", "h30", "f2", "y4", "h31", "t3", "k0", "u0", "k1", "u1", "h40", "h41", "t4",
    "f3", "k2", "u2", "k3", "u3", "u4", "k4",
)


def ring(value, size):
    return lax.rem(value + size, size)


def exchange(
    act_ref, grad_ref, in_basis, out_basis, act_out, grad_out,
    basis, obasis, pair, acts, part, send_y, recv_y, own_y, rot_raw,
    thin, thin_send, thin_recv, thin_own, thin_raw, rot,
    grads, gsend, grecv, gown, gx_send, gx_recv, gsum, ring_send, ring_recv, grot,
    send_sem, recv_sem, local_sem,
):
    row, col = lax.axis_index("row"), lax.axis_index("col")
    z, xl, core = row // 4, lax.rem(row // 2, 2), lax.rem(row, 2)
    y, xh = col // 2, lax.rem(col, 2)

    def at(z=z, xl=xl, core=core, y=y, xh=xh):
        return (z * 4 + xl * 2 + core, y * 2 + xh)

    sibling, beside, across = at(core=1 - core), at(xl=1 - xl), at(xh=1 - xh)
    around = [at(y=ring(y + rel, NY)) for rel in (1, 2, 3)]
    members = [(rel, side) for rel in range(NY) for side in (0, 1)][1:]
    member = {(rel, side): at(y=ring(y + rel, NY), xh=1 - xh if side else xh) for rel, side in members}
    ids, sent, stored = {}, [], []

    def place(zoff):
        return ring(z + zoff, NZ)


    def copy(key, src, dst, device):
        number = ids.setdefault(key, len(ids))
        return pltpu.make_async_remote_copy(
            src_ref=src, dst_ref=dst, send_sem=send_sem.at[number], recv_sem=recv_sem.at[number],
            device_id=device, device_id_type=MESH,
        )

    def send(key, src, dst, device):
        one = copy(key, src, dst, device)
        one.start()
        sent.append(one)

    def arrive(key, dst):
        copy(key, dst, dst, sibling).wait_recv()

    load_basis = pltpu.make_async_copy(in_basis, basis, local_sem.at[8])
    load_obasis = pltpu.make_async_copy(out_basis, obasis, local_sem.at[9])
    load_grads = pltpu.make_async_copy(grad_ref, grads.at[col], local_sem.at[18])
    load_grads.start()
    load_obasis.start()
    load_basis.start()

    barrier = pltpu.get_barrier_semaphore()
    near = [sibling, beside, *(at(z=place(zoff)) for zoff in FAR[:-1]), *member.values()]
    for device in near:
        pl.semaphore_signal(barrier, inc=1, device_id=device, device_id_type=MESH)
    half = act_ref.shape[1] // 2
    quarter = half // 2
    mine = act_ref[...].astype(F32)
    for number in range(2):
        pair[2 + number] = mine[:, number * half : (number + 1) * half]
    pair[core] = pair[2 + core]
    load_grads.wait()
    pl.semaphore_wait(barrier, len(near))

    def act_slot(zz, q, part_no, side=0):
        kk = core if side == 0 else 1 - core
        return acts.at[kk, part_no, zz, xl if q == 0 else 1 - xl]

    def grad_slot(zz, q, part_no, side=0):
        kk = core if side == 0 else 1 - core
        return grot.at[2 * kk + (xl if q == 0 else 1 - xl), zz, pl.ds(96 * part_no, 96)]

    def along(way, hops):
        return at(z=place(hops if way == 0 else -hops))

    def gather_put(name, slot, q, part_no):
        ref = slot(z, q, part_no)
        for way in (0, 1):
            for step in FIRST[name]:
                send((name, way, step, q, part_no), ref, ref, along(way, step))
        if q == 0:
            send((name, "x", part_no), ref, ref, beside)
        send((name, "sib", 0, q, part_no), ref, ref, sibling)

    def gather_beside(name, slot, part_no):
        arrive((name, "x", part_no), slot(z, 1, part_no))
        gather_put(name, slot, 1, part_no)

    def gather_step(name, slot, step, way, q, part_no):
        if step == 4 and part_no != way:
            return
        zoff = 4 if step == 4 else (-step if way == 0 else step)
        ref = slot(place(zoff), q, part_no)
        arrive((name, way, step, q, part_no), ref)
        for later in ONWARD[name].get(step, ()):
            if later < 4 or part_no == way:
                send((name, way, later, q, part_no), ref, ref, along(way, later - step))
        send((name, "sib", zoff, q, part_no), ref, ref, sibling)

    def gather_steps(name, slot, step, q):
        for part_no in (0, 1):
            for way in (0, 1):
                gather_step(name, slot, step, way, q, part_no)

    def gather_sibling(name, slot, zoff):
        for q in (0, 1):
            for part_no in (0, 1):
                arrive((name, "sib", zoff, q, part_no), slot(place(zoff), q, part_no, 1))

    def partial(seq, ref):
        got = jnp.dot(grads[pl.ds(4 * seq, 4)].reshape(384, 256), obasis[...], preferred_element_type=F32)
        for side in range(2):
            for zc in range(NZ):
                ref[side, zc] = got[192 * side : 192 * side + 192, 128 * zc : 128 * zc + 128]

    def rotate(zoffs):
        for zoff in zoffs:
            gather_sibling("a", act_slot, zoff)
        left = jnp.concatenate(
            [
                jnp.concatenate([acts[kk, pp, place(zoff)].reshape(96, quarter) for zoff in zoffs], axis=0)
                for kk in (0, 1)
                for pp in (0, 1)
            ],
            axis=1,
        )
        return jnp.dot(left, basis[...], preferred_element_type=F32)

    def piece_of(wide, yy, hh):
        return (hh, yy) if wide else (2 * lax.rem(yy, 2) + hh, yy // 2)

    def chunk(j):
        zoffs, wide = CHUNKS[j], len(CHUNKS[j]) == 2
        got = rotate(zoffs)
        if wide:
            for n, at_col in enumerate((0, 384)):
                part[n] = got[:, at_col : at_col + 512].reshape(4, 48, 512)
        else:
            for n, at_col in enumerate((0, 256, 512, 640)):
                thin[n] = got[:, at_col : at_col + 256].reshape(2, 48, 256)
        parts, out, came, own = (part, send_y, recv_y, own_y) if wide else (thin, thin_send, thin_recv, thin_own)
        i = SLOT[j]
        for n, (rel, side) in enumerate(members):
            a, b = piece_of(wide, ring(y + rel, NY), 1 - xh if side else xh)
            out[i, n] = parts[a, b].astype(BF16)
            send(("s2", j, n), out.at[i, n], came.at[i, n], member[rel, side])
        a, b = piece_of(wide, y, xh)
        own[i] = parts[a, b]

    def sum_up(j):
        wide, i = len(CHUNKS[j]) == 2, SLOT[j]
        came, own, raw = (recv_y, own_y, rot_raw) if wide else (thin_recv, thin_own, thin_raw)
        total = own[i]
        for n in range(7):
            arrive(("s2", j, n), came.at[i, n])
            total = total + came[i, n].astype(F32)
        raw[i, y, xh] = total.astype(BF16)
        ref = raw.at[i, y, xh]
        if DIRECT[j]:
            for rel, side in members:
                send(("s3", j, rel, side), ref, ref, member[rel, side])
        else:
            send(("s3", j, 0, 1), ref, ref, across)
            for rel in (1, 2, 3):
                send(("s3", j, rel, 0), ref, ref, around[rel - 1])

    def spread_on(j):
        raw = rot_raw if len(CHUNKS[j]) == 2 else thin_raw
        ref = raw.at[SLOT[j], y, 1 - xh]
        arrive(("s3", j, 0, 1), ref)
        if not DIRECT[j]:
            for rel in (1, 2, 3):
                send(("s3", j, rel, 1), ref, ref, around[rel - 1])

    def collect(j):
        zoffs, i = CHUNKS[j], SLOT[j]
        wide = len(zoffs) == 2
        raw = rot_raw if wide else thin_raw
        for rel in (1, 2, 3):
            for side in (0, 1):
                arrive(("s3", j, rel, side), raw.at[i, ring(y - rel, NY), 1 - xh if side else xh])
        if wide:
            whole = jnp.concatenate([raw[i, :, 0], raw[i, :, 1][:, :, 128:]], axis=2)
        else:
            halves = [
                jnp.concatenate(
                    [raw[i, 2 * n, 0], raw[i, 2 * n, 1], raw[i, 2 * n + 1, 0], raw[i, 2 * n + 1, 1][:, 128:]], axis=1
                )
                for n in (0, 1)
            ]
        for n, zoff in enumerate(zoffs):
            zz = place(zoff)
            if wide:
                rot[zz] = whole[2 * n : 2 * n + 2].reshape(96, -1)
            else:
                rot[zz] = jnp.concatenate(halves, axis=0)
            one = pltpu.make_async_copy(rot.at[zz], act_out.at[zz], local_sem.at[zoff + 3])
            one.start()
            stored.append(one)

    def grad_beside():
        arrive(("g2core", 0), grecv.at[1 - xl])
        for zoff in FAR:
            zc = place(zoff)
            gx_send[zc] = (gown[1 - xl, zc] + grecv[1 - xl, zc]).astype(BF16)
            send(("g2x", zoff), gx_send.at[zc], gx_recv.at[zc], beside)
        arrive(("g2core", 1), grecv.at[xl])

    def grad_sum(offsets):
        for zoff in offsets:
            zc = place(zoff)
            arrive(("g2x", zoff), gx_recv.at[zc])
            gsum[zc] = gown[xl, zc] + grecv[xl, zc] + gx_recv[zc].astype(F32)

    def grad_spread(offsets):
        for zoff in offsets:
            n = zoff + 3
            ring_send[n] = gsum[place(zoff)].astype(BF16)
            send(("g2", zoff), ring_send.at[n], ring_recv.at[n], at(z=place(zoff)))

    def grad_end():
        value = gsum[z]
        for zoff in FAR[:-1]:
            arrive(("g2", zoff), ring_recv.at[zoff + 3])
            value = value + ring_recv[zoff + 3].astype(F32)
        grot[2 * core + xl, z] = value.astype(BF16)
        for part_no in (0, 1):
            gather_put("g", grad_slot, 0, part_no)

    def act_pair():
        send("pair", pair.at[3 - core], pair.at[core], sibling)

    def act_start():
        arrive("pair", pair.at[1 - core])
        block = pair[0:2].reshape(48, half).astype(BF16)
        for part_no in (0, 1):
            acts[core, part_no, z, xl] = block[:, part_no * quarter : (part_no + 1) * quarter]
        for part_no in (0, 1):
            gather_put("a", act_slot, 0, part_no)

    def act_beside():
        for part_no in (0, 1):
            gather_beside("a", act_slot, part_no)

    def grad_start():
        send(("g1", 0), grads.at[col], grads.at[col], across)
        for rel in (1, 2, 3):
            send(("g1", rel, 0), grads.at[col], grads.at[col], around[rel - 1])

    def grad_on():
        other = y * 2 + 1 - xh
        arrive(("g1", 0), grads.at[other])
        for rel in (1, 2, 3):
            send(("g1", rel, 1), grads.at[other], grads.at[other], around[rel - 1])

    def grad_partial():
        for rel in (1, 2, 3):
            came = ring(y - rel, NY) * 2
            arrive(("g1", rel, 0), grads.at[came + xh])
            arrive(("g1", rel, 1), grads.at[came + 1 - xh])
        load_obasis.wait()
        partial(1 - core, gsend)
        for n, side in enumerate((1 - xl, xl)):
            send(("g2core", n), gsend.at[side], grecv.at[side], sibling)
        partial(core, gown)

    def grad_gather_start():
        for part_no in (0, 1):
            gather_beside("g", grad_slot, part_no)

    def grad_store(offsets):
        for zoff in offsets:
            gather_sibling("g", grad_slot, zoff)
            zz = place(zoff)
            one = pltpu.make_async_copy(grot.at[:, zz], grad_out.at[:, zz], local_sem.at[zoff + 13])
            one.start()
            stored.append(one)

    def flush():
        while len(sent) > 48:
            sent.pop(0).wait_send()

    steps = {
        "pair": act_pair, "ga": grad_start, "a0": act_start, "gb": grad_on, "ax": act_beside, "gp": grad_partial,
        "gx": grad_beside, "ge": grad_end, "gy": grad_gather_start,
        "basis": load_basis.wait, "f0": flush, "f1": flush, "f2": flush, "f3": flush,
    }
    for n, offsets in enumerate((FAR[:3], FAR[3:5], FAR[5:])):
        steps[f"gs{n}"] = functools.partial(grad_sum, offsets)
    for n in range(4):
        for q in (0, 1):
            steps[f"a{n + 1}{q}"] = functools.partial(gather_steps, "a", act_slot, n + 1, q)
            steps[f"h{n + 1}{q}"] = functools.partial(gather_steps, "g", grad_slot, n + 1, q)
    for n, offsets in enumerate(((0,), (1, -1), (2, -2), (3, -3), (4,))):
        steps[f"k{n}"] = functools.partial(grad_store, offsets)
    for n, offsets in enumerate((FAR[:3], FAR[3:5], FAR[5:7])):
        steps[f"r{n}"] = functools.partial(grad_spread, offsets)
    for n in range(5):
        steps[f"c{n}"] = functools.partial(chunk, n)
        steps[f"y{n}"] = functools.partial(sum_up, n)
        steps[f"t{n}"] = functools.partial(spread_on, n)
        steps[f"u{n}"] = functools.partial(collect, n)
    for name in ORDER:
        steps[name]()
    for one in sent:
        one.wait_send()
    for one in stored:
        one.wait()


def tiles(act_hbm, grad_hbm, out_hbm, act, grad, turned, out, in_sem, out_sem):
    wide = act.shape[2]
    loads = []
    for seq in range(2):
        for n, (src, dst, step) in enumerate(((act_hbm, act, 4), (grad_hbm, grad, 2))):
            rows = pl.ds(step * seq, step)
            loads.append(pltpu.make_async_copy(src.at[rows], dst.at[rows], in_sem.at[2 * seq + n]))
    for one in loads:
        one.start()
    stores = []
    for seq in range(2):
        loads[2 * seq].wait()
        turned[seq] = act[4 * seq : 4 * seq + 4].reshape(384, wide).T
        loads[2 * seq + 1].wait()
    for n in range(4):
        total = None
        for seq in range(2):
            right = jnp.concatenate(
                [grad[2 * seq : 2 * seq + 2, 2 * n + zc].reshape(384, 128) for zc in range(2)], axis=1
            )
            tile = jnp.dot(turned[seq], right, preferred_element_type=F32)
            total = tile * tile if total is None else total + tile * tile
        out[n] = total * F32(0.5)
        one = pltpu.make_async_copy(out.at[n], out_hbm.at[:, pl.ds(256 * n, 256)], out_sem.at[n])
        one.start()
        stores.append(one)
    for one in stores:
        one.wait()


def on_device(activations, out_grads, in_basis, out_basis):
    rows, depth = activations.shape
    wide = in_basis.shape[1]
    vmem = pl.BlockSpec(memory_space=pltpu.VMEM)
    hbm = pl.BlockSpec(memory_space=pl.ANY)
    act_rotated, grad_rotated = pl.pallas_call(
        exchange,
        out_shape=(
            jax.ShapeDtypeStruct((NZ, 96, wide), BF16),
            jax.ShapeDtypeStruct((4, NZ, 192, 128), BF16),
        ),
        in_specs=[vmem, hbm, hbm, hbm],
        out_specs=(hbm, hbm),
        scratch_shapes=[
            pltpu.VMEM(in_basis.shape, BF16),
            pltpu.VMEM(out_basis.shape, BF16),
            pltpu.VMEM((4, rows, depth // 2), F32),
            pltpu.VMEM((2, 2, NZ, 2, 48, depth // 4), BF16),
            pltpu.VMEM((2, NY, 48, 512), F32),
            pltpu.VMEM((3, 7, 48, 512), BF16),
            pltpu.VMEM((3, 7, 48, 512), BF16),
            pltpu.VMEM((3, 48, 512), F32),
            pltpu.VMEM((3, NY, 2, 48, 512), BF16),
            pltpu.VMEM((4, 2, 48, 256), F32),
            pltpu.VMEM((2, 7, 48, 256), BF16),
            pltpu.VMEM((2, 7, 48, 256), BF16),
            pltpu.VMEM((2, 48, 256), F32),
            pltpu.VMEM((2, NY, 2, 48, 256), BF16),
            pltpu.VMEM((NZ, 96, wide), BF16),
            pltpu.VMEM((8, 96, 256), BF16),
            pltpu.VMEM((2, NZ, 192, 128), F32),
            pltpu.VMEM((2, NZ, 192, 128), F32),
            pltpu.VMEM((2, NZ, 192, 128), F32),
            pltpu.VMEM((NZ, 192, 128), BF16),
            pltpu.VMEM((NZ, 192, 128), BF16),
            pltpu.VMEM((NZ, 192, 128), F32),
            pltpu.VMEM((NZ, 192, 128), BF16),
            pltpu.VMEM((NZ, 192, 128), BF16),
            pltpu.VMEM((4, NZ, 192, 128), BF16),
            pltpu.SemaphoreType.DMA((COPIES,)),
            pltpu.SemaphoreType.DMA((COPIES,)),
            pltpu.SemaphoreType.DMA((19,)),
        ],
        compiler_params=pltpu.CompilerParams(
            collective_id=0, has_side_effects=True, vmem_limit_bytes=VMEM_LIMIT
        ),
    )(activations, out_grads, in_basis, out_basis)
    return pl.pallas_call(
        tiles,
        out_shape=jax.ShapeDtypeStruct((wide, 1024), F32),
        in_specs=[hbm, hbm],
        out_specs=hbm,
        scratch_shapes=[
            pltpu.VMEM((NZ, 96, wide), BF16),
            pltpu.VMEM((4, NZ, 192, 128), BF16),
            pltpu.VMEM((2, wide, 384), BF16),
            pltpu.VMEM((4, wide, 256), F32),
            pltpu.SemaphoreType.DMA((4,)),
            pltpu.SemaphoreType.DMA((4,)),
        ],
        compiler_params=pltpu.CompilerParams(vmem_limit_bytes=VMEM_LIMIT),
    )(act_rotated, grad_rotated)


def solution(mesh):
    placed = (P("row", "col"), P("col", "row"), P("col", "row"), P("row", "col"))
    return jax.shard_map(
        on_device, mesh=mesh, in_specs=placed, out_specs=P("row", "col"), check_vma=False
    )
```
